32 devices in a mesh: groups: 2 (over y), feat: 4 (over z), node: 4 (over x, core).
Axes of the slice: x: 2, y: 2, z: 4, core: 2. Of those that a mesh axis runs over, the one named last changes fastest.
Arguments:
- features: bfloat16 [32768, 768], P(('groups', 'node'), 'feat'), parts along dimension 0, may hold values from -6 to 6
- intra_tiles: int32 [256, 3], P(('groups', 'node')), parts along dimension 0, may hold values from 0 to 31, all different within a row
- intra_values: bfloat16 [256, 3, 128, 128], P(('groups', 'node')), parts along dimension 0, may hold values from -0.3125 to 0.3125
- cut_tiles: int32 [256, 1], P(('groups', 'node')), parts along dimension 0, may hold values from 0 to 7
- cut_values: bfloat16 [256, 1, 128, 128], P(('groups', 'node')), parts along dimension 0, may hold values from -0.5 to 0.5
- send_rows: int32 [8, 4, 256], P(('groups', 'node')), parts along dimension 0, may hold values from 0 to 4095
- halo_counts: int32 [8, 4], P('groups'), parts along dimension 0, may hold values from 0 to 256, as said below
- self_l1: bfloat16 [768, 1024], replicated, may hold values from -0.21875 to 0.21875
- neigh_l1: bfloat16 [768, 1024], replicated, may hold values from -0.21875 to 0.21875
- self_l2: bfloat16 [1024, 153], replicated, may hold values from -0.1875 to 0.1875
- neigh_l2: bfloat16 [1024, 153], replicated, may hold values from -0.1875 to 0.1875
Outputs:
- logits: bfloat16 [32768, 153], P(('groups', 'node', 'feat')), parts along dimension 0
The draws below stay inside these ranges and needn't reach their ends.
There are 2 independent parts, one for each index of `groups`. The reference program is written for one: setup_inputs(seed, part) draws one part's arguments, and reference() takes and returns one part's arrays. A program takes and returns all parts, laid end to end along the dimension named above; an argument that names none is the same for every part. Nothing has to cross between parts.
Inputs may be any that keep to these rules, and one draw needn't show every extreme that they name: `halo_counts`: the diagonal is 0; in every draw some reader block receives 256 live slots from every other block.
All inputs are finite; a program needn't handle non-finite values.
Results may differ from the reference program's by a relative error of at most 0.0055.
Values may be sent and summed in bfloat16 or wider, within the bound.
A program may use at most 128 MiB of HBM per device.

```python
import jax
import jax.numpy as jnp
from jax import lax

FEAT_IN = 768
HIDDEN_SIZE = 1024
CLASSES = 153
TILE_SIZE = 128
INTRA_K = 3
CUT_K = 1
HALO_SLOTS = 256
BLOCK_ROWS = 4096
BATCH_NODES = 16384
ROW_TILES = 32
N_NODE = 4


def draw_halo_counts(key, part):
    key = jax.random.fold_in(key, 5)
    first_key, second_key = jax.random.split(key)
    counts = jax.random.randint(first_key, (N_NODE, N_NODE), HALO_SLOTS // 4, HALO_SLOTS + 1)
    busiest = jax.random.randint(second_key, (), 0, N_NODE)
    column = jnp.arange(N_NODE)
    counts = jnp.where(column[None, :] == busiest, HALO_SLOTS, counts)
    counts = jnp.where(column[:, None] == column[None, :], 0, counts)
    return counts.astype(jnp.int32)


def set_ends(result, own_key, low, top_value):
    longest = result.shape.index(max(result.shape))
    spots = []
    for shift in (0, 1):
        where = [jax.random.randint(jax.random.fold_in(own_key, axis), (), 0, length) for axis, length in enumerate(result.shape)]
        where[longest] = (where[longest] + shift) % result.shape[longest]
        spots.append(tuple(where))
    return result.at[spots[0]].set(low).at[spots[1]].set(top_value)


def shard_levels(rng, dims, pieces, smallest, top_value):
    gain = 1.0
    for position, parts in pieces:
        draws = jax.random.uniform(jax.random.fold_in(jax.random.fold_in(rng, 6), position), (parts,), jnp.float32, smallest / len(pieces), top_value / len(pieces))
        gain = gain * jnp.repeat(jnp.exp(draws), dims[position] // parts).reshape((-1,) + (1,) * (len(dims) - 1 - position))
    return gain


def different_ones(stream_key, rows, number_of, top, lift):
    sequence = jax.random.permutation(jax.random.fold_in(stream_key, 1), number_of)
    boost = sequence
    for power in range(3):
        boost = boost * boost // number_of
    boost = boost * lift // number_of
    tickets = jax.random.randint(jax.random.fold_in(stream_key, 2), (rows, number_of), 0, 4096) + boost
    fixed_rows = jax.random.permutation(jax.random.fold_in(stream_key, 3), rows)[jnp.arange(number_of) % rows]
    tickets = jnp.where(jnp.arange(rows)[:, None] == fixed_rows[None, :], 1 << 14, tickets)
    score = tickets * number_of + jnp.arange(number_of)
    return lax.top_k(score.astype(jnp.int32), top)[1].astype(jnp.int32)


def noise(stream_key, dims, spread, limit, cuts=(), held_as=jnp.bfloat16):
    values = jax.random.normal(stream_key, dims, jnp.float32) * spread
    if len(cuts) > 0:
        values = shard_levels(stream_key, dims, cuts, -0.22, 0.18) * values
    return jnp.clip(values, min=-limit, max=limit).astype(held_as)


def setup_inputs(seed: int = 0, part: int = 0) -> dict:
    keys = jax.random.split(jax.random.key(seed), 12)
    part_keys = jax.random.split(jax.random.fold_in(keys[11], part), 12)
    return {
        "features": noise(part_keys[0], (BATCH_NODES, FEAT_IN), 1.0, 6.0, ((0, 4), (1, 4))),
        "intra_tiles": different_ones(part_keys[1], (N_NODE * ROW_TILES), ROW_TILES, INTRA_K, 0),
        "intra_values": noise(part_keys[2], (N_NODE * ROW_TILES, INTRA_K, TILE_SIZE, TILE_SIZE), (INTRA_K * TILE_SIZE) ** -0.5, 0.3125, ((0, 4),)),
        "cut_tiles": different_ones(part_keys[3], (N_NODE * ROW_TILES), N_NODE * HALO_SLOTS // TILE_SIZE, CUT_K, 0),
        "cut_values": noise(part_keys[4], (N_NODE * ROW_TILES, CUT_K, TILE_SIZE, TILE_SIZE), (CUT_K * TILE_SIZE) ** -0.5, 0.5, ((0, 4),)),
        "send_rows": set_ends(jax.random.randint(part_keys[5], (N_NODE, N_NODE, HALO_SLOTS), 0, BLOCK_ROWS), jax.random.fold_in(part_keys[5], 1), 0, BLOCK_ROWS - 1).astype(jnp.int32),
        "halo_counts": draw_halo_counts(jax.random.fold_in(jax.random.fold_in(keys[11], part), 71), part),
        "self_l1": noise(keys[7], (FEAT_IN, HIDDEN_SIZE), FEAT_IN ** -0.5, 0.21875),
        "neigh_l1": noise(keys[8], (FEAT_IN, HIDDEN_SIZE), FEAT_IN ** -0.5, 0.21875),
        "self_l2": noise(keys[9], (HIDDEN_SIZE, CLASSES), HIDDEN_SIZE ** -0.5, 0.1875),
        "neigh_l2": noise(keys[10], (HIDDEN_SIZE, CLASSES), HIDDEN_SIZE ** -0.5, 0.1875),
    }


def aggregate(tiles, values, source):
    picked = jnp.take(source, tiles, axis=0)
    return jnp.einsum('rkij,rkjw->riw', values.astype(jnp.float32), picked.astype(jnp.float32), precision=lax.Precision.HIGHEST)


def reference(features, intra_tiles, intra_values, cut_tiles, cut_values, send_rows, halo_counts, self_l1, neigh_l1, self_l2, neigh_l2):
    feat_blocks = features.reshape(N_NODE, ROW_TILES, TILE_SIZE, FEAT_IN)
    tile_blocks = intra_tiles.reshape(N_NODE, ROW_TILES, INTRA_K)
    value_blocks = intra_values.reshape(N_NODE, ROW_TILES, INTRA_K, TILE_SIZE, TILE_SIZE)

    def first_layer(items):
        tiles, values, source = items
        return aggregate(tiles, values, source)

    agg1 = lax.map(first_layer, (tile_blocks, value_blocks, feat_blocks))
    agg1 = agg1.reshape(BATCH_NODES, FEAT_IN).astype(jnp.bfloat16)
    pre = jnp.dot(features, self_l1, preferred_element_type=jnp.float32) + jnp.dot(agg1, neigh_l1, preferred_element_type=jnp.float32)
    hidden = jax.nn.relu(pre).astype(jnp.bfloat16)
    hidden_blocks = hidden.reshape(N_NODE, BLOCK_ROWS, HIDDEN_SIZE)
    slot_index = jnp.arange(HALO_SLOTS).astype(jnp.int32)
    live = slot_index[None, None, :] < halo_counts[:, :, None]
    sent = jax.vmap(lambda rows, picks: jnp.take(rows, picks, axis=0))(hidden_blocks, send_rows)
    sent = jnp.where(live[:, :, :, None], sent, jnp.zeros_like(sent))
    received = jnp.swapaxes(sent, 0, 1).reshape(N_NODE, N_NODE * HALO_SLOTS // TILE_SIZE, TILE_SIZE, HIDDEN_SIZE)
    cut_tile_blocks = cut_tiles.reshape(N_NODE, ROW_TILES, CUT_K)
    cut_value_blocks = cut_values.reshape(N_NODE, ROW_TILES, CUT_K, TILE_SIZE, TILE_SIZE)

    def second_layer(items):
        tiles, values, source, ctiles, cvalues, halo = items
        inner = aggregate(tiles, values, source.reshape(ROW_TILES, TILE_SIZE, HIDDEN_SIZE))
        return inner + aggregate(ctiles, cvalues, halo)

    agg2 = lax.map(second_layer, (tile_blocks, value_blocks, hidden_blocks, cut_tile_blocks, cut_value_blocks, received))
    agg2 = agg2.reshape(BATCH_NODES, HIDDEN_SIZE)
    logits = jnp.dot(hidden, self_l2, preferred_element_type=jnp.float32) + jnp.dot(agg2, neigh_l2.astype(jnp.float32), precision=lax.Precision.HIGHEST)
    return logits.astype(jnp.bfloat16)
```

```python
import jax
import jax.numpy as jnp
from jax import lax
from jax.experimental import pallas as pl
from jax.experimental.pallas import tpu as pltpu
from jax.sharding import PartitionSpec as P

MESH = pl.DeviceIdType.MESH
CHUNKS = 2


def pack(x, lanes):
    groups = 128 // lanes
    height = x.shape[0] // groups
    tail = x[:, 128 : 128 + lanes]
    folded = jnp.concatenate([tail[q * height : (q + 1) * height] for q in range(groups)], axis=1)
    return jnp.concatenate([x[:, :128], folded], axis=0)


def unfold(folded, lanes):
    groups = 128 // lanes
    return jnp.concatenate(
        [folded[:, q * lanes : (q + 1) * lanes] for q in range(groups)], axis=0
    )


def kernel(
    intra_t, cut_t, send_rows,
    feats_h, vals_h, cvals_h, w1s_h, w1n_h, w2_h,
    out_ref,
    feats, vals, cvals, w1, w2, pk, rv, acc, hid, own, gath, flat, blocks, hrows, hsend, hrecv, hflat,
    lsem, s1, r1, s2, r2, s3, r3,
):
    z, n = lax.axis_index("feat"), lax.axis_index("node")
    nz, nn = lax.axis_size("feat"), lax.axis_size("node")
    tiles, ts, width = feats.shape
    rest = width - 128
    own_tiles = tiles // nz
    ct = own_tiles // CHUNKS
    intra_k = vals.shape[1]
    slots = send_rows.shape[-1]
    htiles = slots // ts
    classes = out_ref.shape[-1]
    f32, bf16 = jnp.float32, jnp.bfloat16

    local = [
        pltpu.make_async_copy(feats_h, feats, lsem.at[0]),
        pltpu.make_async_copy(vals_h, vals, lsem.at[1]),
        pltpu.make_async_copy(w1s_h, w1.at[0], lsem.at[2]),
        pltpu.make_async_copy(w1n_h, w1.at[1], lsem.at[3]),
        pltpu.make_async_copy(w2_h, w2, lsem.at[4]),
        pltpu.make_async_copy(cvals_h, cvals, lsem.at[5]),
    ]
    for copy in local:
        copy.start()

    barrier = pltpu.get_barrier_semaphore()
    for off in range(1, nz):
        pl.semaphore_signal(barrier, inc=1, device_id={"feat": lax.rem(z + off, nz)}, device_id_type=MESH)
    for off in range(1, nn):
        pl.semaphore_signal(barrier, inc=1, device_id={"node": lax.rem(n + off, nn)}, device_id_type=MESH)
    local[0].wait()

    def pack_feats(t):
        pk[0, t] = pack(feats[t].astype(f32), rest).astype(bf16)

    def pack_agg(t):
        picked = jnp.concatenate([feats[intra_t[t, k]] for k in range(intra_k)], axis=0)
        weights = jnp.concatenate([vals[t, k] for k in range(intra_k)], axis=1)
        total = jnp.dot(weights, picked, preferred_element_type=f32)
        pk[1, t] = pack(total, rest).astype(bf16)

    def l1_copy(kind, off, c):
        to = lax.rem(z + off, nz)
        return pltpu.make_async_remote_copy(
            src_ref=pk.at[kind, pl.ds(to * own_tiles + c * ct, ct)],
            dst_ref=rv.at[kind, z, pl.ds(c * ct, ct)],
            send_sem=s1.at[kind, off - 1, c],
            recv_sem=r1.at[kind, off - 1, c],
            device_id={"feat": to},
            device_id_type=MESH,
        )

    order = [2, 1, 3] if nz == 4 else list(range(1, nz))
    for c in range(CHUNKS):
        for kind in range(2):
            if c == 0 and kind == 1:
                local[1].wait()
            for off in order + [0]:
                to = lax.rem(z + off, nz)
                base = to * own_tiles + c * ct

                def step(i, _, kind=kind, base=base):
                    (pack_feats if kind == 0 else pack_agg)(base + i)
                    return 0

                lax.fori_loop(0, ct, step, 0)
                if off == 0:
                    rv[kind, z, c * ct : (c + 1) * ct] = pk[kind, pl.ds(base, ct)]
                else:
                    if c == 0 and kind == 0 and off == order[0]:
                        pl.semaphore_wait(barrier, nz - 1 + nn - 1)
                    l1_copy(kind, off, c).start()
    for copy in local[2:]:
        copy.wait()

    def accumulate(kind, source, c, first=False):
        rows = []
        for i in range(ct):
            record = rv[kind, source, c * ct + i]
            tail = unfold(record[ts:].astype(f32), rest).astype(bf16)
            rows.append(jnp.concatenate([record[:ts], tail], axis=1))
        lhs = jnp.concatenate(rows, axis=0)
        part = jnp.dot(lhs, w1[kind, source], preferred_element_type=f32)
        if first:
            acc[...] = part
        else:
            acc[...] += part

    def from_others(kind, c):
        def step(off, _):
            l1_copy(kind, off, c).wait_recv()
            accumulate(kind, lax.rem(z + nz - off, nz), c)
            return 0

        lax.fori_loop(1, nz, step, 0)

    def ag_copy(c, right, k):
        source = z - k if right else z + k
        piece = gath.at[pl.ds(source * own_tiles + c * ct, ct)]
        side = 1 if right else 0
        return pltpu.make_async_remote_copy(
            src_ref=piece,
            dst_ref=piece,
            send_sem=s2.at[c, side, k],
            recv_sem=r2.at[c, side, k],
            device_id={"feat": z + 1 if right else z - 1},
            device_id_type=MESH,
        )

    def ag_send(c, k):
        @pl.when((z - k >= 0) & (z + 1 < nz))
        def _():
            ag_copy(c, True, k).start()

        @pl.when((z + k < nz) & (z >= 1))
        def _():
            ag_copy(c, False, k).start()

    def ag_sent(c, k):
        @pl.when((z - k >= 0) & (z + 1 < nz))
        def _():
            ag_copy(c, True, k).wait_send()

        @pl.when((z + k < nz) & (z >= 1))
        def _():
            ag_copy(c, False, k).wait_send()

    def flatten(source, c):
        def step(i, _):
            t = source * own_tiles + c * ct + i
            record = gath[t]
            tail = unfold(record[ts:].astype(f32), 32)
            rows = pl.ds(pl.multiple_of(t * ts, ts), ts)
            flat[rows, :128] = record[:ts].astype(f32)
            flat[rows, 128:160] = tail
            blocks[t, :, :128] = record[:ts]
            blocks[t, :, 128:160] = tail.astype(bf16)
            return 0

        lax.fori_loop(0, ct, step, 0)

    def ag_step(c, k):
        def arrived(right, source):
            piece = gath.at[pl.ds(source * own_tiles + c * ct, ct)]
            side = 1 if right else 0
            pltpu.make_async_copy(piece, piece, r2.at[c, side, k - 1]).wait()

        @pl.when(z - k >= 0)
        def _():
            arrived(True, z - k)

            @pl.when(z + 1 < nz)
            def _():
                if k < nz - 1:
                    ag_copy(c, True, k).start()

        @pl.when(z + k < nz)
        def _():
            arrived(False, z + k)

            @pl.when(z >= 1)
            def _():
                if k < nz - 1:
                    ag_copy(c, False, k).start()

        @pl.when(z - k >= 0)
        def _():
            flatten(z - k, c)

        @pl.when(z + k < nz)
        def _():
            flatten(z + k, c)

    flat[:, 128:] = jnp.zeros((flat.shape[0], 128), f32)
    flat[tiles * ts :, :128] = jnp.zeros((8, 128), f32)
    blocks[:, :, 128:] = jnp.zeros((tiles, ts, 128), bf16)

    def project(c):
        hid[...] = jnp.maximum(acc[...], 0.0).astype(bf16)
        both = jnp.dot(hid[...], w2[...], preferred_element_type=f32)
        own[c * ct * ts : (c + 1) * ct * ts, :] = both[:, 256:]
        for i in range(ct):
            gath[z * own_tiles + c * ct + i] = pack(
                both[i * ts : (i + 1) * ts, :256], 32
            ).astype(bf16)
        ag_send(c, 0)
        flatten(z, c)

    for c in range(CHUNKS):
        accumulate(0, z, c, first=True)
        accumulate(1, z, c)
        from_others(0, c)
        if c > 0:
            ag_step(c - 1, 1)
        from_others(1, c)
        project(c)
        if c > 0:
            for k in range(2, nz):
                ag_step(c - 1, k)
    for k in range(1, nz):
        ag_step(CHUNKS - 1, k)

    def h_copy(off):
        to = lax.rem(n + off, nn)
        return pltpu.make_async_remote_copy(
            src_ref=hsend.at[off - 1],
            dst_ref=hrecv.at[n],
            send_sem=s3.at[off - 1],
            recv_sem=r3.at[off - 1],
            device_id={"node": to},
            device_id_type=MESH,
        )

    for off in range(1, nn):
        to = lax.rem(n + off, nn)

        def pick(i, _, to=to):
            for u in range(16):
                j = i * 16 + u
                hrows[j] = flat[send_rows[0, to, j]]
            return 0

        lax.fori_loop(0, slots // 16, pick, 0)
        for h in range(htiles):
            hsend[off - 1, h] = pack(hrows[h * ts : (h + 1) * ts, :], 32).astype(bf16)
        h_copy(off).start()

    hflat[...] = jnp.zeros_like(hflat)

    def inner(i, _):
        t = z * own_tiles + i
        picked = jnp.concatenate(
            [blocks[intra_t[t, k]] for k in range(intra_k)], axis=0
        )
        weights = jnp.concatenate([vals[t, k] for k in range(intra_k)], axis=1)
        rows = pl.ds(pl.multiple_of(i * ts, ts), ts)
        own[rows, :] += jnp.dot(weights, picked, preferred_element_type=f32)
        return 0

    lax.fori_loop(0, own_tiles, inner, 0)

    for off in range(1, nn):
        h_copy(off).wait_recv()
        source = lax.rem(n + nn - off, nn)
        for h in range(htiles):
            record = hrecv[source, h]
            t = source * htiles + h
            hflat[t, :, :128] = record[:ts]
            hflat[t, :, 128:160] = unfold(record[ts:].astype(f32), 32).astype(bf16)

    def outer(i, _):
        t = z * own_tiles + i
        rows = pl.ds(pl.multiple_of(i * ts, ts), ts)
        total = own[rows, :]
        for k in range(cvals.shape[1]):
            total += jnp.dot(cvals[t, k], hflat[cut_t[t, k]], preferred_element_type=f32)
        out_ref[rows, :] = total[:, :classes].astype(bf16)
        return 0

    lax.fori_loop(0, own_tiles, outer, 0)

    for c in range(CHUNKS):
        for kind in range(2):
            for off in range(1, nz):
                l1_copy(kind, off, c).wait_send()
        for k in range(nz - 1):
            ag_sent(c, k)
    for off in range(1, nn):
        h_copy(off).wait_send()


def fused(
    features, intra_tiles, intra_values, cut_tiles, cut_values, send_rows, halo_counts,
    self_l1, neigh_l1, self_l2, neigh_l2,
):
    nz, nn = lax.axis_size("feat"), lax.axis_size("node")
    block_rows, width = features.shape
    ts = intra_values.shape[-1]
    tiles = block_rows // ts
    own_rows = block_rows // nz
    own_tiles = tiles // nz
    hidden = self_l1.shape[1]
    classes = self_l2.shape[1]
    slots = send_rows.shape[-1]
    htiles = slots // ts
    pad = ((0, 0), (0, 256 - classes))
    w2 = jnp.concatenate([jnp.pad(neigh_l2, pad), jnp.pad(self_l2, pad)], axis=1)
    leaving = halo_counts[lax.axis_index("node")]
    rows = jnp.where(jnp.arange(slots)[None, None, :] < leaving[None, :, None], send_rows, block_rows)
    record = ts + ts * (width - 128) // 128
    ct = own_tiles // CHUNKS
    bf16, f32 = jnp.bfloat16, jnp.float32
    smem = pl.BlockSpec(memory_space=pltpu.SMEM)
    hbm = pl.BlockSpec(memory_space=pl.ANY)
    dma = pltpu.SemaphoreType.DMA
    return pl.pallas_call(
        kernel,
        out_shape=jax.ShapeDtypeStruct((own_rows, classes), bf16),
        in_specs=[smem] * 3 + [hbm] * 6,
        out_specs=pl.BlockSpec(memory_space=pltpu.VMEM),
        scratch_shapes=[
            pltpu.VMEM((tiles, ts, width), bf16),
            pltpu.VMEM(intra_values.shape, bf16),
            pltpu.VMEM(cut_values.shape, bf16),
            pltpu.VMEM((2, nz, width, hidden), bf16),
            pltpu.VMEM((hidden, 512), bf16),
            pltpu.VMEM((2, tiles, record, 128), bf16),
            pltpu.VMEM((2, nz, own_tiles, record, 128), bf16),
            pltpu.VMEM((ct * ts, hidden), f32),
            pltpu.VMEM((ct * ts, hidden), bf16),
            pltpu.VMEM((own_rows, 256), f32),
            pltpu.VMEM((tiles, ts + ts // 4, 128), bf16),
            pltpu.VMEM((block_rows + 8, 256), f32),
            pltpu.VMEM((tiles, ts, 256), bf16),
            pltpu.VMEM((slots, 256), f32),
            pltpu.VMEM((nn - 1, htiles, ts + ts // 4, 128), bf16),
            pltpu.VMEM((nn, htiles, ts + ts // 4, 128), bf16),
            pltpu.VMEM((nn * htiles, ts, 256), bf16),
            dma((6,)),
            dma((2, nz - 1, CHUNKS)),
            dma((2, nz - 1, CHUNKS)),
            dma((CHUNKS, 2, nz - 1)),
            dma((CHUNKS, 2, nz - 1)),
            dma((nn - 1,)),
            dma((nn - 1,)),
        ],
        compiler_params=pltpu.CompilerParams(
            collective_id=0, has_side_effects=True, vmem_limit_bytes=56 * 1024 * 1024
        ),
    )(
        intra_tiles, cut_tiles, rows,
        features.reshape(tiles, ts, width), intra_values, cut_values,
        self_l1.reshape(nz, width, hidden), neigh_l1.reshape(nz, width, hidden), w2,
    )


def tile_sum(tiles, values, source):
    picked = jnp.take(source, tiles, axis=0)
    return jnp.einsum(
        "rkij,rkjw->riw",
        values,
        picked,
        preferred_element_type=jnp.float32,
        precision=lax.Precision.HIGHEST,
    )


def shards(
    features,
    intra_tiles,
    intra_values,
    cut_tiles,
    cut_values,
    send_rows,
    halo_counts,
    self_l1,
    neigh_l1,
    self_l2,
    neigh_l2,
):
    parts = lax.axis_size("feat")
    block_rows, slice_width = features.shape
    if slice_width == 192 and block_rows <= 4096 and 128 < self_l2.shape[1] <= 160:
        return fused(
            features, intra_tiles, intra_values, cut_tiles, cut_values, send_rows, halo_counts,
            self_l1, neigh_l1, self_l2, neigh_l2,
        )
    tile_size = intra_values.shape[-1]
    row_tiles = block_rows // tile_size
    own_rows = block_rows // parts
    slots = send_rows.shape[-1]
    classes = self_l2.shape[1]
    feat_tiles = features.reshape(row_tiles, tile_size, slice_width)
    agg1 = (
        tile_sum(intra_tiles, intra_values, feat_tiles)
        .reshape(block_rows, slice_width)
        .astype(jnp.bfloat16)
    )
    feat_rows = lax.all_to_all(
        features.reshape(parts, own_rows, slice_width),
        "feat",
        split_axis=0,
        concat_axis=2,
        tiled=True,
    )
    agg_rows = lax.all_to_all(
        agg1.reshape(parts, own_rows, slice_width), "feat", split_axis=0, concat_axis=2, tiled=True
    )
    pre = jnp.dot(feat_rows[0], self_l1, preferred_element_type=jnp.float32)
    pre = pre + jnp.dot(agg_rows[0], neigh_l1, preferred_element_type=jnp.float32)
    hidden = jax.nn.relu(pre).astype(jnp.bfloat16)[None][0]
    here = lax.axis_index("node")
    arriving = lax.dynamic_index_in_dim(halo_counts, here, axis=1, keepdims=False)
    live = jnp.arange(slots)[None, :] < arriving[:, None]
    projected = jnp.dot(hidden, neigh_l2, preferred_element_type=jnp.float32)
    block_proj = lax.all_gather(projected, "feat", axis=0, tiled=True)
    outgoing = jnp.take(block_proj, send_rows[0], axis=0)
    incoming = lax.all_to_all(outgoing, "node", split_axis=0, concat_axis=0, tiled=True)
    incoming = jnp.where(live[:, :, None], incoming, 0.0).reshape(-1, tile_size, classes)
    own_tiles = own_rows // tile_size
    first_tile = lax.axis_index("feat") * own_tiles
    my_tiles = lax.dynamic_slice_in_dim(intra_tiles, first_tile, own_tiles, 0)
    my_values = lax.dynamic_slice_in_dim(intra_values, first_tile, own_tiles, 0).astype(jnp.float32)
    my_cut_tiles = lax.dynamic_slice_in_dim(cut_tiles, first_tile, own_tiles, 0)
    my_cut_values = lax.dynamic_slice_in_dim(cut_values, first_tile, own_tiles, 0).astype(
        jnp.float32
    )
    inner = tile_sum(my_tiles, my_values, block_proj.reshape(row_tiles, tile_size, classes))
    outer = tile_sum(my_cut_tiles, my_cut_values, incoming)
    neighbour = (inner + outer).reshape(own_rows, classes)
    logits = jnp.dot(hidden, self_l2, preferred_element_type=jnp.float32) + neighbour
    return logits.astype(jnp.bfloat16)


def solution(mesh):
    placed = (
        P(("groups", "node"), "feat"),
        P(("groups", "node"), None),
        P(("groups", "node"), None, None, None),
        P(("groups", "node"), None),
        P(("groups", "node"), None, None, None),
        P(("groups", "node"), None, None),
        P("groups", None),
        P(),
        P(),
        P(),
        P(),
    )
    return jax.shard_map(
        shards,
        mesh=mesh,
        in_specs=placed,
        out_specs=P(("groups", "node", "feat"), None),
        check_vma=False,
    )
```

```python
import jax
import jax.numpy as jnp
from jax import lax
from jax.experimental import pallas as pl
from jax.experimental.pallas import tpu as pltpu
from jax.sharding import PartitionSpec as P

MESH = pl.DeviceIdType.MESH
CHUNKS = 2
F32, BF16 = jnp.float32, jnp.bfloat16


def dot(a, b, left, right):
    return lax.dot_general(a, b, (((left,), (right,)), ((), ())), preferred_element_type=F32)


def kernel(
    intra_t, cut_t, send_rows, counts,
    feats_h, vals_h, cvals_h, w1s_h, w1n_h, w2n_h, w2s_h,
    out_ref,
    whole, feats, vals, cvals, w1, w2n, w2s, agg, rv, acc, proj, own, gath, flat, hrows, hsend, hrecv,
    lsem, s1, r1, s2, r2, s3, r3,
):
    z, n = lax.axis_index("feat"), lax.axis_index("node")
    nz, nn = lax.axis_size("feat"), lax.axis_size("node")
    tiles, width, ts = feats.shape
    own_tiles = tiles // nz
    ct = own_tiles // CHUNKS
    part = ct * ts
    intra_k = vals.shape[1]
    slots = send_rows.shape[-1]
    htiles = slots // ts
    classes = out_ref.shape[0]

    local = [
        pltpu.make_async_copy(feats_h, whole, lsem.at[0]),
        pltpu.make_async_copy(vals_h, vals, lsem.at[1]),
        pltpu.make_async_copy(w1s_h, w1.at[0], lsem.at[2]),
        pltpu.make_async_copy(w1n_h, w1.at[1], lsem.at[3]),
        pltpu.make_async_copy(w2n_h, w2n, lsem.at[4]),
        pltpu.make_async_copy(w2s_h, w2s, lsem.at[5]),
        pltpu.make_async_copy(cvals_h, cvals, lsem.at[6]),
    ]
    for copy in local:
        copy.start()

    barrier = pltpu.get_barrier_semaphore()
    for off in range(1, nz):
        pl.semaphore_signal(barrier, inc=1, device_id={"feat": lax.rem(z + off, nz)}, device_id_type=MESH)
    for off in range(1, nn):
        pl.semaphore_signal(barrier, inc=1, device_id={"node": lax.rem(n + off, nn)}, device_id_type=MESH)
    local[0].wait()
    pl.semaphore_wait(barrier, nz - 1 + nn - 1)

    def l1_copy(kind, off, c):
        to = lax.rem(z + off, nz)
        if kind == 0:
            start = pl.multiple_of((to * CHUNKS + c) * part, part)
            source = whole.at[:, pl.ds(start, part)]
        else:
            source = agg.at[to, c]
        return pltpu.make_async_remote_copy(
            src_ref=source,
            dst_ref=rv.at[kind, z, c],
            send_sem=s1.at[kind, off - 1, c],
            recv_sem=r1.at[kind, off - 1, c],
            device_id={"feat": to},
            device_id_type=MESH,
        )

    order = [2, 1, 3] if nz == 4 else list(range(1, nz))
    for off in order:
        l1_copy(0, off, 0).start()
    for t in range(tiles):
        feats[t] = whole[:, t * ts : (t + 1) * ts]

    def aggregate(to, c):
        for i in range(ct):
            t = (to * CHUNKS + c) * ct + i
            picked = jnp.concatenate([feats[intra_t[k, t]] for k in range(intra_k)], axis=1)
            weights = jnp.concatenate([vals[t, k] for k in range(intra_k)], axis=1)
            agg[to, c, :, i * ts : (i + 1) * ts] = dot(picked, weights, 1, 1).astype(BF16)

    local[1].wait()
    for c in range(CHUNKS):
        if c > 0:
            for off in order:
                l1_copy(0, off, c).start()
        for off in order:
            aggregate(lax.rem(z + off, nz), c)
            l1_copy(1, off, c).start()
    for c in range(CHUNKS):
        aggregate(z, c)
    for copy in local[2:]:
        copy.wait()

    def accumulate(kind, source, block, first=False):
        term = dot(w1[kind, source], block, 0, 0)
        if first:
            acc[...] = term
        else:
            acc[...] += term

    def from_others(kind, c):
        def step(off, _):
            l1_copy(kind, off, c).wait_recv()
            source = lax.rem(z + nz - off, nz)
            accumulate(kind, source, rv[kind, source, c])
            return 0

        lax.fori_loop(1, nz, step, 0)

    def ag_piece(source, c):
        return gath.at[pl.ds(source * own_tiles + c * ct, ct)]

    def ag_copy(c, right, k):
        piece = ag_piece(z - k if right else z + k, c)
        side = 1 if right else 0
        return pltpu.make_async_remote_copy(
            src_ref=piece,
            dst_ref=piece,
            send_sem=s2.at[c, side, k],
            recv_sem=r2.at[c, side, k],
            device_id={"feat": z + 1 if right else z - 1},
            device_id_type=MESH,
        )

    def ag_send(c, k):
        @pl.when((z - k >= 0) & (z + 1 < nz))
        def _():
            ag_copy(c, True, k).start()

        @pl.when((z + k < nz) & (z >= 1))
        def _():
            ag_copy(c, False, k).start()

    def ag_sent(c, k):
        @pl.when((z - k >= 0) & (z + 1 < nz))
        def _():
            ag_copy(c, True, k).wait_send()

        @pl.when((z + k < nz) & (z >= 1))
        def _():
            ag_copy(c, False, k).wait_send()

    def flatten(source, c):
        for i in range(ct):
            t = source * own_tiles + c * ct + i
            rows = pl.ds(pl.multiple_of(t * ts, ts), ts)
            tile = gath[t].astype(F32)
            flat[rows, :128] = tile[:128].T
            flat[rows, 128:160] = tile[128:].T

    def ag_step(c, k):
        @pl.when(z - k >= 0)
        def _():
            piece = ag_piece(z - k, c)
            pltpu.make_async_copy(piece, piece, r2.at[c, 1, k - 1]).wait()
            if k < nz - 1:
                @pl.when(z + 1 < nz)
                def _():
                    ag_copy(c, True, k).start()

        @pl.when(z + k < nz)
        def _():
            piece = ag_piece(z + k, c)
            pltpu.make_async_copy(piece, piece, r2.at[c, 0, k - 1]).wait()
            if k < nz - 1:
                @pl.when(z >= 1)
                def _():
                    ag_copy(c, False, k).start()

        @pl.when(z - k >= 0)
        def _():
            flatten(z - k, c)

        @pl.when(z + k < nz)
        def _():
            flatten(z + k, c)

    proj[...] = jnp.zeros_like(proj)
    own[...] = jnp.zeros_like(own)
    flat[:, 128:] = jnp.zeros((flat.shape[0], 128), F32)

    def project(c):
        hidden = jnp.maximum(acc[...], 0.0).astype(BF16)
        proj[:classes, :] = dot(w2n[...], hidden, 1, 0)
        for i in range(ct):
            gath[z * own_tiles + c * ct + i] = proj[:, i * ts : (i + 1) * ts].astype(BF16)
        ag_send(c, 0)
        own[:classes, c * part : (c + 1) * part] = dot(w2s[...], hidden, 1, 0)
        flatten(z, c)

    for c in range(CHUNKS):
        start = pl.multiple_of((z * CHUNKS + c) * part, part)
        accumulate(0, z, whole[:, pl.ds(start, part)], first=True)
        accumulate(1, z, agg[z, c])
        from_others(0, c)
        if c > 0:
            ag_step(c - 1, 1)
        from_others(1, c)
        project(c)
        if c > 0:
            for k in range(2, nz):
                ag_step(c - 1, k)
    for k in range(1, nz):
        ag_step(CHUNKS - 1, k)

    def h_copy(off):
        return pltpu.make_async_remote_copy(
            src_ref=hsend.at[off - 1],
            dst_ref=hrecv.at[pl.ds(n * htiles, htiles)],
            send_sem=s3.at[off - 1],
            recv_sem=r3.at[off - 1],
            device_id={"node": lax.rem(n + off, nn)},
            device_id_type=MESH,
        )

    for off in range(1, nn):
        to = lax.rem(n + off, nn)

        def pick(i, _, to=to):
            for u in range(16):
                j = i * 16 + u
                hrows[j] = flat[send_rows[0, to, j]]
            return 0

        lax.fori_loop(0, slots // 16, pick, 0)
        slot = lax.broadcasted_iota(jnp.int32, (1, ts), 1)
        for h in range(htiles):
            live = jnp.clip(counts[n, to] - h * ts - slot, 0, 1).astype(F32)
            rows = hrows[h * ts : (h + 1) * ts, :].T
            hsend[off - 1, h] = (rows[:160] * live).astype(BF16)
        h_copy(off).start()
    hrecv[pl.ds(n * htiles, htiles)] = jnp.zeros((htiles,) + hrecv.shape[1:], BF16)

    for i in range(own_tiles):
        t = z * own_tiles + i
        picked = jnp.concatenate([gath[intra_t[k, t]] for k in range(intra_k)], axis=1)
        weights = jnp.concatenate([vals[t, k] for k in range(intra_k)], axis=1)
        own[:, i * ts : (i + 1) * ts] += dot(picked, weights, 1, 1)

    for off in range(1, nn):
        h_copy(off).wait_recv()
    for i in range(own_tiles):
        t = z * own_tiles + i
        total = own[:, i * ts : (i + 1) * ts]
        for k in range(cvals.shape[1]):
            total += dot(hrecv[cut_t[k, t]], cvals[t, k], 1, 1)
        out_ref[:, i * ts : (i + 1) * ts] = total[:classes].astype(BF16)

    for c in range(CHUNKS):
        for kind in range(2):
            for off in range(1, nz):
                l1_copy(kind, off, c).wait_send()
        for k in range(nz - 1):
            ag_sent(c, k)
    for off in range(1, nn):
        h_copy(off).wait_send()


def fused(
    features, intra_tiles, intra_values, cut_tiles, cut_values, send_rows, halo_counts,
    self_l1, neigh_l1, self_l2, neigh_l2,
):
    nz, nn = lax.axis_size("feat"), lax.axis_size("node")
    block_rows, width = features.shape
    ts = intra_values.shape[-1]
    tiles = block_rows // ts
    own_rows = block_rows // nz
    own_tiles = tiles // nz
    hidden = self_l1.shape[1]
    classes = self_l2.shape[1]
    slots = send_rows.shape[-1]
    htiles = slots // ts
    ct = own_tiles // CHUNKS
    part = ct * ts
    smem = pl.BlockSpec(memory_space=pltpu.SMEM)
    hbm = pl.BlockSpec(memory_space=pl.ANY)
    dma = pltpu.SemaphoreType.DMA
    vmem = pltpu.VMEM
    out = pl.pallas_call(
        kernel,
        out_shape=jax.ShapeDtypeStruct((classes, own_rows), BF16),
        in_specs=[smem] * 4 + [hbm] * 7,
        out_specs=pl.BlockSpec(memory_space=pltpu.VMEM),
        scratch_shapes=[
            vmem((width, block_rows), BF16),
            vmem((tiles, width, ts), BF16),
            vmem(intra_values.shape, BF16),
            vmem(cut_values.shape, BF16),
            vmem((2, nz, width, hidden), BF16),
            vmem((classes, hidden), BF16),
            vmem((classes, hidden), BF16),
            vmem((nz, CHUNKS, width, part), BF16),
            vmem((2, nz, CHUNKS, width, part), BF16),
            vmem((hidden, part), F32),
            vmem((160, part), F32),
            vmem((160, own_rows), F32),
            vmem((tiles, 160, ts), BF16),
            vmem((block_rows, 256), F32),
            vmem((slots, 256), F32),
            vmem((nn - 1, htiles, 160, ts), BF16),
            vmem((nn * htiles, 160, ts), BF16),
            dma((7,)),
            dma((2, nz - 1, CHUNKS)),
            dma((2, nz - 1, CHUNKS)),
            dma((CHUNKS, 2, nz - 1)),
            dma((CHUNKS, 2, nz - 1)),
            dma((nn - 1,)),
            dma((nn - 1,)),
        ],
        compiler_params=pltpu.CompilerParams(
            collective_id=0, has_side_effects=True, vmem_limit_bytes=56 * 1024 * 1024
        ),
    )(
        intra_tiles.T, cut_tiles.T, send_rows, halo_counts,
        features.T, intra_values, cut_values,
        self_l1.reshape(nz, width, hidden), neigh_l1.reshape(nz, width, hidden),
        neigh_l2.T, self_l2.T,
    )
    return out.T


def tile_sum(tiles, values, source):
    picked = jnp.take(source, tiles, axis=0)
    return jnp.einsum(
        "rkij,rkjw->riw",
        values,
        picked,
        preferred_element_type=jnp.float32,
        precision=lax.Precision.HIGHEST,
    )


def shards(
    features,
    intra_tiles,
    intra_values,
    cut_tiles,
    cut_values,
    send_rows,
    halo_counts,
    self_l1,
    neigh_l1,
    self_l2,
    neigh_l2,
):
    parts = lax.axis_size("feat")
    block_rows, slice_width = features.shape
    if slice_width == 192 and block_rows <= 4096 and 128 < self_l2.shape[1] <= 160:
        return fused(
            features, intra_tiles, intra_values, cut_tiles, cut_values, send_rows, halo_counts,
            self_l1, neigh_l1, self_l2, neigh_l2,
        )
    tile_size = intra_values.shape[-1]
    row_tiles = block_rows // tile_size
    own_rows = block_rows // parts
    slots = send_rows.shape[-1]
    classes = self_l2.shape[1]
    feat_tiles = features.reshape(row_tiles, tile_size, slice_width)
    agg1 = (
        tile_sum(intra_tiles, intra_values, feat_tiles)
        .reshape(block_rows, slice_width)
        .astype(jnp.bfloat16)
    )
    feat_rows = lax.all_to_all(
        features.reshape(parts, own_rows, slice_width),
        "feat",
        split_axis=0,
        concat_axis=2,
        tiled=True,
    )
    agg_rows = lax.all_to_all(
        agg1.reshape(parts, own_rows, slice_width), "feat", split_axis=0, concat_axis=2, tiled=True
    )
    pre = jnp.dot(feat_rows[0], self_l1, preferred_element_type=jnp.float32)
    pre = pre + jnp.dot(agg_rows[0], neigh_l1, preferred_element_type=jnp.float32)
    hidden = jax.nn.relu(pre).astype(jnp.bfloat16)[None][0]
    here = lax.axis_index("node")
    arriving = lax.dynamic_index_in_dim(halo_counts, here, axis=1, keepdims=False)
    live = jnp.arange(slots)[None, :] < arriving[:, None]
    projected = jnp.dot(hidden, neigh_l2, preferred_element_type=jnp.float32)
    block_proj = lax.all_gather(projected, "feat", axis=0, tiled=True)
    outgoing = jnp.take(block_proj, send_rows[0], axis=0)
    incoming = lax.all_to_all(outgoing, "node", split_axis=0, concat_axis=0, tiled=True)
    incoming = jnp.where(live[:, :, None], incoming, 0.0).reshape(-1, tile_size, classes)
    own_tiles = own_rows // tile_size
    first_tile = lax.axis_index("feat") * own_tiles
    my_tiles = lax.dynamic_slice_in_dim(intra_tiles, first_tile, own_tiles, 0)
    my_values = lax.dynamic_slice_in_dim(intra_values, first_tile, own_tiles, 0).astype(jnp.float32)
    my_cut_tiles = lax.dynamic_slice_in_dim(cut_tiles, first_tile, own_tiles, 0)
    my_cut_values = lax.dynamic_slice_in_dim(cut_values, first_tile, own_tiles, 0).astype(
        jnp.float32
    )
    inner = tile_sum(my_tiles, my_values, block_proj.reshape(row_tiles, tile_size, classes))
    outer = tile_sum(my_cut_tiles, my_cut_values, incoming)
    neighbour = (inner + outer).reshape(own_rows, classes)
    logits = jnp.dot(hidden, self_l2, preferred_element_type=jnp.float32) + neighbour
    return logits.astype(jnp.bfloat16)


def solution(mesh):
    placed = (
        P(("groups", "node"), "feat"),
        P(("groups", "node"), None),
        P(("groups", "node"), None, None, None),
        P(("groups", "node"), None),
        P(("groups", "node"), None, None, None),
        P(("groups", "node"), None, None),
        P("groups", None),
        P(),
        P(),
        P(),
        P(),
    )
    return jax.shard_map(
        shards,
        mesh=mesh,
        in_specs=placed,
        out_specs=P(("groups", "node", "feat"), None),
        check_vma=False,
    )
```

```python
import jax
import jax.numpy as jnp
from jax import lax
from jax.experimental import pallas as pl
from jax.experimental.pallas import tpu as pltpu
from jax.sharding import PartitionSpec as P

MESH = pl.DeviceIdType.MESH
CHUNKS = 2
PIECES = 2 * CHUNKS
F32, BF16 = jnp.float32, jnp.bfloat16


def dot(a, b, left, right):
    return lax.dot_general(a, b, (((left,), (right,)), ((), ())), preferred_element_type=F32)


def kernel(
    intra_t, cut_t, send_rows, counts,
    feats_h, vals_h, cvals_h, w1s_h, w1n_h, w2n_h, w2s_h,
    out_ref,
    whole, feats, vals, cvals, w1, w2n, w2s, agg, rv, acc, proj, own, gath, flat, hrows, hsend, hrecv,
    lsem, s1, r1, s2, r2, s3, r3,
):
    z, n = lax.axis_index("feat"), lax.axis_index("node")
    nz, nn = lax.axis_size("feat"), lax.axis_size("node")
    tiles, width, ts = feats.shape
    own_tiles = tiles // nz
    ct = own_tiles // CHUNKS
    pt = own_tiles // PIECES
    part = ct * ts
    intra_k = vals.shape[1]
    slots = send_rows.shape[-1]
    htiles = slots // ts
    classes = out_ref.shape[0]

    local = [
        pltpu.make_async_copy(feats_h, whole, lsem.at[0]),
        pltpu.make_async_copy(vals_h, vals, lsem.at[1]),
        pltpu.make_async_copy(w1s_h, w1.at[0], lsem.at[2]),
        pltpu.make_async_copy(w1n_h, w1.at[1], lsem.at[3]),
        pltpu.make_async_copy(w2n_h, w2n, lsem.at[4]),
        pltpu.make_async_copy(w2s_h, w2s, lsem.at[5]),
        pltpu.make_async_copy(cvals_h, cvals, lsem.at[6]),
    ]
    for copy in local:
        copy.start()

    barrier = pltpu.get_barrier_semaphore()
    for off in range(1, nz):
        pl.semaphore_signal(barrier, inc=1, device_id={"feat": lax.rem(z + off, nz)}, device_id_type=MESH)
    for off in range(1, nn):
        pl.semaphore_signal(barrier, inc=1, device_id={"node": lax.rem(n + off, nn)}, device_id_type=MESH)
    local[0].wait()
    pl.semaphore_wait(barrier, nz - 1 + nn - 1)

    def l1_copy(kind, off, c):
        to = lax.rem(z + off, nz)
        if kind == 0:
            start = pl.multiple_of((to * CHUNKS + c) * part, part)
            source = whole.at[:, pl.ds(start, part)]
        else:
            source = agg.at[to, c]
        return pltpu.make_async_remote_copy(
            src_ref=source,
            dst_ref=rv.at[kind, z, c],
            send_sem=s1.at[kind, off - 1, c],
            recv_sem=r1.at[kind, off - 1, c],
            device_id={"feat": to},
            device_id_type=MESH,
        )

    order = [2, 1, 3] if nz == 4 else list(range(1, nz))
    for off in order:
        l1_copy(0, off, 0).start()
    for t in range(tiles):
        feats[t] = whole[:, t * ts : (t + 1) * ts]

    def aggregate(to, c):
        for i in range(ct):
            t = (to * CHUNKS + c) * ct + i
            picked = jnp.concatenate([feats[intra_t[k, t]] for k in range(intra_k)], axis=1)
            weights = jnp.concatenate([vals[t, k] for k in range(intra_k)], axis=1)
            agg[to, c, :, i * ts : (i + 1) * ts] = dot(picked, weights, 1, 1).astype(BF16)

    local[1].wait()
    for c in range(CHUNKS):
        if c > 0:
            for off in order:
                l1_copy(0, off, c).start()
        for off in order:
            aggregate(lax.rem(z + off, nz), c)
            l1_copy(1, off, c).start()
    for c in range(CHUNKS):
        aggregate(z, c)
    for copy in local[2:]:
        copy.wait()

    def accumulate(kind, source, block, first=False):
        term = dot(w1[kind, source], block, 0, 0)
        if first:
            acc[...] = term
        else:
            acc[...] += term

    def from_others(kind, c):
        def step(off, _):
            l1_copy(kind, off, c).wait_recv()
            source = lax.rem(z + nz - off, nz)
            accumulate(kind, source, rv[kind, source, c])
            return 0

        lax.fori_loop(1, nz, step, 0)

    def ag_piece(source, c):
        return gath.at[pl.ds(source * own_tiles + c * pt, pt)]

    def ag_copy(c, right, k):
        piece = ag_piece(z - k if right else z + k, c)
        side = 1 if right else 0
        return pltpu.make_async_remote_copy(
            src_ref=piece,
            dst_ref=piece,
            send_sem=s2.at[c, side, k],
            recv_sem=r2.at[c, side, k],
            device_id={"feat": z + 1 if right else z - 1},
            device_id_type=MESH,
        )

    def ag_send(c, k):
        @pl.when((z - k >= 0) & (z + 1 < nz))
        def _():
            ag_copy(c, True, k).start()

        @pl.when((z + k < nz) & (z >= 1))
        def _():
            ag_copy(c, False, k).start()

    def ag_sent(c, k):
        @pl.when((z - k >= 0) & (z + 1 < nz))
        def _():
            ag_copy(c, True, k).wait_send()

        @pl.when((z + k < nz) & (z >= 1))
        def _():
            ag_copy(c, False, k).wait_send()

    def flatten(source, c):
        for i in range(pt):
            t = source * own_tiles + c * pt + i
            rows = pl.ds(pl.multiple_of(t * ts, ts), ts)
            tile = gath[t].astype(F32)
            flat[rows, :128] = tile[:128].T
            flat[rows, 128:160] = tile[128:].T

    def ag_step(c, k):
        @pl.when(z - k >= 0)
        def _():
            piece = ag_piece(z - k, c)
            pltpu.make_async_copy(piece, piece, r2.at[c, 1, k - 1]).wait()
            if k < nz - 1:
                @pl.when(z + 1 < nz)
                def _():
                    ag_copy(c, True, k).start()

        @pl.when(z + k < nz)
        def _():
            piece = ag_piece(z + k, c)
            pltpu.make_async_copy(piece, piece, r2.at[c, 0, k - 1]).wait()
            if k < nz - 1:
                @pl.when(z >= 1)
                def _():
                    ag_copy(c, False, k).start()

        @pl.when(z - k >= 0)
        def _():
            flatten(z - k, c)

        @pl.when(z + k < nz)
        def _():
            flatten(z + k, c)

    def pieces(c):
        return range(c * (PIECES // CHUNKS), (c + 1) * (PIECES // CHUNKS))

    proj[...] = jnp.zeros_like(proj)
    own[...] = jnp.zeros_like(own)
    flat[:, 128:] = jnp.zeros((flat.shape[0], 128), F32)

    def project(c):
        hidden = jnp.maximum(acc[...], 0.0).astype(BF16)
        proj[:classes, :] = dot(w2n[...], hidden, 1, 0)
        for i in range(ct):
            gath[z * own_tiles + c * ct + i] = proj[:, i * ts : (i + 1) * ts].astype(BF16)
        for p in pieces(c):
            ag_send(p, 0)
        own[:classes, c * part : (c + 1) * part] = dot(w2s[...], hidden, 1, 0)
        for p in pieces(c):
            flatten(z, p)

    for c in range(CHUNKS):
        start = pl.multiple_of((z * CHUNKS + c) * part, part)
        accumulate(0, z, whole[:, pl.ds(start, part)], first=True)
        accumulate(1, z, agg[z, c])
        from_others(0, c)
        if c > 0:
            for p in pieces(c - 1):
                ag_step(p, 1)
        from_others(1, c)
        project(c)
        if c > 0:
            for k in range(2, nz):
                for p in pieces(c - 1):
                    ag_step(p, k)
    for k in range(1, nz):
        for p in pieces(CHUNKS - 1):
            ag_step(p, k)

    def h_copy(off):
        return pltpu.make_async_remote_copy(
            src_ref=hsend.at[off - 1],
            dst_ref=hrecv.at[pl.ds(n * htiles, htiles)],
            send_sem=s3.at[off - 1],
            recv_sem=r3.at[off - 1],
            device_id={"node": lax.rem(n + off, nn)},
            device_id_type=MESH,
        )

    for off in range(1, nn):
        to = lax.rem(n + off, nn)

        def pick(i, _, to=to):
            for u in range(16):
                j = i * 16 + u
                hrows[j] = flat[send_rows[0, to, j]]
            return 0

        lax.fori_loop(0, slots // 16, pick, 0)
        slot = lax.broadcasted_iota(jnp.int32, (1, ts), 1)
        for h in range(htiles):
            live = jnp.clip(counts[n, to] - h * ts - slot, 0, 1).astype(F32)
            rows = hrows[h * ts : (h + 1) * ts, :].T
            hsend[off - 1, h] = (rows[:160] * live).astype(BF16)
        h_copy(off).start()
    hrecv[pl.ds(n * htiles, htiles)] = jnp.zeros((htiles,) + hrecv.shape[1:], BF16)

    for i in range(own_tiles):
        t = z * own_tiles + i
        picked = jnp.concatenate([gath[intra_t[k, t]] for k in range(intra_k)], axis=1)
        weights = jnp.concatenate([vals[t, k] for k in range(intra_k)], axis=1)
        own[:, i * ts : (i + 1) * ts] += dot(picked, weights, 1, 1)

    for off in range(1, nn):
        h_copy(off).wait_recv()
    for i in range(own_tiles):
        t = z * own_tiles + i
        total = own[:, i * ts : (i + 1) * ts]
        for k in range(cvals.shape[1]):
            total += dot(hrecv[cut_t[k, t]], cvals[t, k], 1, 1)
        out_ref[:, i * ts : (i + 1) * ts] = total[:classes].astype(BF16)

    for c in range(CHUNKS):
        for kind in range(2):
            for off in range(1, nz):
                l1_copy(kind, off, c).wait_send()
        for k in range(nz - 1):
            for p in pieces(c):
                ag_sent(p, k)
    for off in range(1, nn):
        h_copy(off).wait_send()


def fused(
    features, intra_tiles, intra_values, cut_tiles, cut_values, send_rows, halo_counts,
    self_l1, neigh_l1, self_l2, neigh_l2,
):
    nz, nn = lax.axis_size("feat"), lax.axis_size("node")
    block_rows, width = features.shape
    ts = intra_values.shape[-1]
    tiles = block_rows // ts
    own_rows = block_rows // nz
    own_tiles = tiles // nz
    hidden = self_l1.shape[1]
    classes = self_l2.shape[1]
    slots = send_rows.shape[-1]
    htiles = slots // ts
    ct = own_tiles // CHUNKS
    part = ct * ts
    smem = pl.BlockSpec(memory_space=pltpu.SMEM)
    hbm = pl.BlockSpec(memory_space=pl.ANY)
    dma = pltpu.SemaphoreType.DMA
    vmem = pltpu.VMEM
    out = pl.pallas_call(
        kernel,
        out_shape=jax.ShapeDtypeStruct((classes, own_rows), BF16),
        in_specs=[smem] * 4 + [hbm] * 7,
        out_specs=pl.BlockSpec(memory_space=pltpu.VMEM),
        scratch_shapes=[
            vmem((width, block_rows), BF16),
            vmem((tiles, width, ts), BF16),
            vmem(intra_values.shape, BF16),
            vmem(cut_values.shape, BF16),
            vmem((2, nz, width, hidden), BF16),
            vmem((classes, hidden), BF16),
            vmem((classes, hidden), BF16),
            vmem((nz, CHUNKS, width, part), BF16),
            vmem((2, nz, CHUNKS, width, part), BF16),
            vmem((hidden, part), F32),
            vmem((160, part), F32),
            vmem((160, own_rows), F32),
            vmem((tiles, 160, ts), BF16),
            vmem((block_rows, 256), F32),
            vmem((slots, 256), F32),
            vmem((nn - 1, htiles, 160, ts), BF16),
            vmem((nn * htiles, 160, ts), BF16),
            dma((7,)),
            dma((2, nz - 1, CHUNKS)),
            dma((2, nz - 1, CHUNKS)),
            dma((PIECES, 2, nz - 1)),
            dma((PIECES, 2, nz - 1)),
            dma((nn - 1,)),
            dma((nn - 1,)),
        ],
        compiler_params=pltpu.CompilerParams(
            collective_id=0, has_side_effects=True, vmem_limit_bytes=56 * 1024 * 1024
        ),
    )(
        intra_tiles.T, cut_tiles.T, send_rows, halo_counts,
        features.T, intra_values, cut_values,
        self_l1.reshape(nz, width, hidden), neigh_l1.reshape(nz, width, hidden),
        neigh_l2.T, self_l2.T,
    )
    return out.T


def tile_sum(tiles, values, source):
    picked = jnp.take(source, tiles, axis=0)
    return jnp.einsum(
        "rkij,rkjw->riw",
        values,
        picked,
        preferred_element_type=jnp.float32,
        precision=lax.Precision.HIGHEST,
    )


def shards(
    features,
    intra_tiles,
    intra_values,
    cut_tiles,
    cut_values,
    send_rows,
    halo_counts,
    self_l1,
    neigh_l1,
    self_l2,
    neigh_l2,
):
    parts = lax.axis_size("feat")
    block_rows, slice_width = features.shape
    if slice_width == 192 and block_rows <= 4096 and 128 < self_l2.shape[1] <= 160:
        return fused(
            features, intra_tiles, intra_values, cut_tiles, cut_values, send_rows, halo_counts,
            self_l1, neigh_l1, self_l2, neigh_l2,
        )
    tile_size = intra_values.shape[-1]
    row_tiles = block_rows // tile_size
    own_rows = block_rows // parts
    slots = send_rows.shape[-1]
    classes = self_l2.shape[1]
    feat_tiles = features.reshape(row_tiles, tile_size, slice_width)
    agg1 = (
        tile_sum(intra_tiles, intra_values, feat_tiles)
        .reshape(block_rows, slice_width)
        .astype(jnp.bfloat16)
    )
    feat_rows = lax.all_to_all(
        features.reshape(parts, own_rows, slice_width),
        "feat",
        split_axis=0,
        concat_axis=2,
        tiled=True,
    )
    agg_rows = lax.all_to_all(
        agg1.reshape(parts, own_rows, slice_width), "feat", split_axis=0, concat_axis=2, tiled=True
    )
    pre = jnp.dot(feat_rows[0], self_l1, preferred_element_type=jnp.float32)
    pre = pre + jnp.dot(agg_rows[0], neigh_l1, preferred_element_type=jnp.float32)
    hidden = jax.nn.relu(pre).astype(jnp.bfloat16)[None][0]
    here = lax.axis_index("node")
    arriving = lax.dynamic_index_in_dim(halo_counts, here, axis=1, keepdims=False)
    live = jnp.arange(slots)[None, :] < arriving[:, None]
    projected = jnp.dot(hidden, neigh_l2, preferred_element_type=jnp.float32)
    block_proj = lax.all_gather(projected, "feat", axis=0, tiled=True)
    outgoing = jnp.take(block_proj, send_rows[0], axis=0)
    incoming = lax.all_to_all(outgoing, "node", split_axis=0, concat_axis=0, tiled=True)
    incoming = jnp.where(live[:, :, None], incoming, 0.0).reshape(-1, tile_size, classes)
    own_tiles = own_rows // tile_size
    first_tile = lax.axis_index("feat") * own_tiles
    my_tiles = lax.dynamic_slice_in_dim(intra_tiles, first_tile, own_tiles, 0)
    my_values = lax.dynamic_slice_in_dim(intra_values, first_tile, own_tiles, 0).astype(jnp.float32)
    my_cut_tiles = lax.dynamic_slice_in_dim(cut_tiles, first_tile, own_tiles, 0)
    my_cut_values = lax.dynamic_slice_in_dim(cut_values, first_tile, own_tiles, 0).astype(
        jnp.float32
    )
    inner = tile_sum(my_tiles, my_values, block_proj.reshape(row_tiles, tile_size, classes))
    outer = tile_sum(my_cut_tiles, my_cut_values, incoming)
    neighbour = (inner + outer).reshape(own_rows, classes)
    logits = jnp.dot(hidden, self_l2, preferred_element_type=jnp.float32) + neighbour
    return logits.astype(jnp.bfloat16)


def solution(mesh):
    placed = (
        P(("groups", "node"), "feat"),
        P(("groups", "node"), None),
        P(("groups", "node"), None, None, None),
        P(("groups", "node"), None),
        P(("groups", "node"), None, None, None),
        P(("groups", "node"), None, None),
        P("groups", None),
        P(),
        P(),
        P(),
        P(),
    )
    return jax.shard_map(
        shards,
        mesh=mesh,
        in_specs=placed,
        out_specs=P(("groups", "node", "feat"), None),
        check_vma=False,
    )
```
